32 devices in a mesh: groups: 2 (over y), expert: 4 (over z), rep: 4 (over x, core).
Axes of the slice: x: 2, y: 2, z: 4, core: 2. Of those that a mesh axis runs over, the one named last changes fastest.
Arguments:
- tokens: bfloat16 [128, 4096], P(('groups', 'expert', 'rep')), parts along dimension 0, may hold values from -6 to 6
- expert_ids: int32 [128, 8], P(('groups', 'expert', 'rep')), parts along dimension 0, may hold values from 0 to 31, as said below
- route_probs: float32 [128, 8], P(('groups', 'expert', 'rep')), parts along dimension 0, may hold values from 0.3 to 1
- gate_weight: bfloat16 [32, 1536, 4096], P('expert', 'rep'), may hold values from -0.09375 to 0.09375
- up_weight: bfloat16 [32, 1536, 4096], P('expert', 'rep'), may hold values from -0.09375 to 0.09375
- down_weight: bfloat16 [32, 1536, 4096], P('expert', 'rep'), may hold values from -0.15625 to 0.15625
Outputs:
- moe_out: bfloat16 [128, 4096], P(('groups', 'expert', 'rep')), parts along dimension 0
The draws below stay inside these ranges and needn't reach their ends.
There are 2 independent parts, one for each index of `groups`. The reference program is written for one: setup_inputs(seed, part) draws one part's arguments, and reference() takes and returns one part's arrays. A program takes and returns all parts, laid end to end along the dimension named above; an argument that names none is the same for every part. Nothing has to cross between parts.
Inputs may be any that keep to these rules, and one draw needn't show every extreme that they name: `expert_ids`: each row names 8 different experts. Among the rows of one device no expert is named more than 3 times, and some expert is named exactly 3 times among the rows of every device.
All inputs are finite; a program needn't handle non-finite values.
Results may differ from the reference program's by a relative error of at most 0.0058.
Values may be sent and summed in bfloat16 or wider, within the bound.
No kernel may reach another device: no remote copies, remote signals or barrier semaphores. Data moves between devices by JAX's collectives and lax.ppermute only.
A program may use at most 128 MiB of HBM per device.

```python
import math
import jax
import jax.numpy as jnp
from jax import lax

D = 4096
FF = 1536
TOPK = 8
EXPERTS = 32
TOK_DEV = 4
CAP = 3
HID_DEV = 384
TOKENS = 64


def draw_expert_ids(key, part):
    block_count = TOKENS // TOK_DEV
    mean_load = TOK_DEV * TOPK // EXPERTS
    capacity = 3 * mean_load
    group_count = EXPERTS // 4
    hottest = jax.random.randint(jax.random.fold_in(key, 7), (), 0, EXPERTS)

    def draw_block(block_key):
        key_list = jax.random.split(block_key, 5)
        ranking = jax.random.permutation(key_list[0], jnp.arange(EXPERTS, dtype=jnp.int32))
        located = jnp.argmax(ranking == hottest)
        leading = ranking[0]
        ranking = ranking.at[located].set(leading).at[0].set(hottest)
        cut_first = jax.random.randint(key_list[1], (group_count,), 0, mean_load + 1)
        cut_second = jax.random.randint(key_list[2], (group_count,), 0, mean_load + 1)
        lower_cut = jnp.minimum(cut_first, cut_second)
        upper_cut = jnp.maximum(cut_first, cut_second)
        heavy_loads = jnp.stack([jnp.full((group_count,), capacity, jnp.int32), lower_cut, upper_cut - lower_cut, mean_load - upper_cut], axis=1)
        shifts = jax.random.randint(key_list[3], (group_count, 2), -mean_load, mean_load + 1)
        even_loads = jnp.stack([mean_load + shifts[:, 0], mean_load - shifts[:, 0], mean_load + shifts[:, 1], mean_load - shifts[:, 1]], axis=1)
        leader = jax.random.randint(key_list[4], (group_count,), 0, 4) == 0
        leader = leader.at[0].set(True)
        load_list = jnp.where(leader[:, None], heavy_loads, even_loads).reshape(-1).astype(jnp.int32)
        run_ends = jnp.cumsum(load_list)
        positions = jnp.arange(TOK_DEV * TOPK, dtype=jnp.int32)
        run_index = jnp.searchsorted(run_ends, positions, side='right')
        chosen = ranking[run_index]
        return chosen.reshape(TOPK, TOK_DEV).T
    block_keys = jax.random.split(jax.random.fold_in(key, 11), block_count)
    return jax.vmap(draw_block)(block_keys).reshape(TOKENS, TOPK).astype(jnp.int32)


def steps_of(stream_key, dims, cuts, smallest, top_value):
    def one(dim, shards_of):
        steps = jax.random.uniform(jax.random.fold_in(jax.random.fold_in(stream_key, 6), dim), (shards_of,), jnp.float32, smallest / len(cuts), top_value / len(cuts))
        return jnp.repeat(jnp.exp(steps), dims[dim] // shards_of).reshape((-1,) + (1,) * (len(dims) - dim - 1))

    factor_of = one(*cuts[0])
    for cut in cuts[1:]:
        factor_of = factor_of * one(*cut)
    return factor_of


def normal_values(own_key, dims, deviation, bound, cuts=(), held_as=jnp.bfloat16):
    gain = steps_of(own_key, dims, cuts, -0.22, 0.18) if cuts else 1.0
    entries = jax.random.normal(own_key, dims, jnp.float32) * deviation * gain
    return jnp.minimum(jnp.maximum(entries, -bound), bound).astype(held_as)


def setup_inputs(seed: int = 0, part: int = 0) -> dict:
    splits = jax.random.split(jax.random.key(seed), 7)
    part_splits = jax.random.split(jax.random.fold_in(splits[6], part), 7)
    tokens = normal_values(part_splits[0], (TOKENS, D), 1.0, 6.0, ((0, 16),))
    expert_ids = draw_expert_ids(jax.random.fold_in(jax.random.fold_in(splits[6], part), 71), part)
    route_probs = jnp.clip(jnp.exp(math.log(1.0) - 1.2039728 * jax.random.uniform(part_splits[2], (TOKENS, TOPK), jnp.float32) ** steps_of(part_splits[2], (TOKENS, TOPK), ((0, 16),), -0.2, 0.2)), 0.3, 1.0)
    gate_weight = normal_values(splits[3], (EXPERTS, FF, D), D ** -0.5, 0.09375, ((0, 4), (1, 4)))
    up_weight = normal_values(splits[4], (EXPERTS, FF, D), D ** -0.5, 0.09375, ((0, 4), (1, 4)))
    down_weight = normal_values(splits[5], (EXPERTS, FF, D), FF ** -0.5, 0.15625, ((0, 4), (1, 4)))
    return {"tokens": tokens, "expert_ids": expert_ids, "route_probs": route_probs, "gate_weight": gate_weight, "up_weight": up_weight, "down_weight": down_weight}


def slot_numbers(route_ids):
    flat_ids = route_ids.reshape(-1)
    one_hot = (flat_ids[:, None] == jnp.arange(EXPERTS, dtype=jnp.int32)[None, :]).astype(jnp.int32)
    running = jnp.cumsum(one_hot, axis=0)
    return (jnp.sum(running * one_hot, axis=1) - 1).astype(jnp.int32).reshape(route_ids.shape)


def expert_rows(row_block, w_gate, w_up, w_down):
    gate_proj = jnp.dot(row_block, w_gate.T, preferred_element_type=jnp.float32)
    up_proj = jnp.dot(row_block, w_up.T, preferred_element_type=jnp.float32)
    hidden = (jax.nn.silu(gate_proj) * up_proj).astype(jnp.bfloat16)
    slices = FF // HID_DEV
    pieces = hidden.reshape(row_block.shape[0], slices, HID_DEV).astype(jnp.float32)
    down_pieces = w_down.reshape(slices, HID_DEV, D).astype(jnp.float32)
    slice_parts = jnp.einsum("rsh,shd->srd", pieces, down_pieces)
    rounded = lax.optimization_barrier(slice_parts.astype(jnp.bfloat16))
    return jnp.sum(rounded.astype(jnp.float32), axis=0)


def reference(tokens, expert_ids, route_probs, gate_weight, up_weight, down_weight):
    block_count = TOKENS // TOK_DEV
    block_ids = expert_ids.reshape(block_count, TOK_DEV, TOPK)
    slots = jax.vmap(slot_numbers)(block_ids)
    blocks = jnp.arange(block_count, dtype=jnp.int32)[:, None, None]
    row_span = block_count * CAP
    slot_place = (block_ids * row_span + blocks * CAP + slots).astype(jnp.int32).reshape(TOKENS, TOPK)
    buffer = jnp.zeros((EXPERTS * row_span, D), jnp.bfloat16)
    buffer = buffer.at[slot_place.reshape(-1)].set(jnp.repeat(tokens, TOPK, axis=0))
    outputs = lax.map(lambda packed: expert_rows(*packed),
                      (buffer.reshape(EXPERTS, row_span, D), gate_weight, up_weight, down_weight))
    flat_out = outputs.reshape(EXPERTS * row_span, D)
    weights = route_probs / jnp.sum(route_probs, axis=1, keepdims=True)
    combined = jnp.zeros((TOKENS, D), jnp.float32)
    for column in range(TOPK):
        combined = combined + weights[:, column:column + 1] * flat_out[slot_place[:, column]]
    return combined.astype(jnp.bfloat16)
```

```python
import functools

import jax
import jax.numpy as jnp
from jax import lax
from jax.experimental import pallas as pl
from jax.experimental.pallas import tpu as pltpu
from jax.sharding import PartitionSpec as P

LANES = 128
PACK = 16
ROW_TILE = 128
VMEM_BYTES = 64 * 2**20
EARLY_CHUNKS = 5
RING_CHUNKS = 10
NT = (((1,), (1,)), ((), ()))
LINKED = ("expert", "rep")
VMEM = pl.BlockSpec(memory_space=pltpu.VMEM)
HBM = pl.BlockSpec(memory_space=pltpu.HBM)


def chip_pairs(chips):
    return [(k + 1, k) if k + 2 == chips else (k, k + 1) for k in range(chips - 2, 0, -2)], 1


def chip_perm(chips, first, second):
    return [
        (chip * 2 + core, ((chip ^ (second if core else first)) << 1) | core)
        for chip in range(chips)
        for core in (0, 1)
    ]


def core_perm(chips):
    return [(device, device ^ 1) for device in range(2 * chips)]


def in_vmem(array):
    return pltpu.with_memory_space_constraint(array, pltpu.VMEM)


def padded_lanes(experts):
    return -(-2 * experts // LANES) * LANES


def rows_kernel(experts, tokens_in, ids_in, probs_in, rows_ref, tokens_ref, ids_ref, probs_ref, sem):
    width = tokens_ref.shape[1]
    copies = [
        pltpu.make_async_copy(source, target, sem.at[index])
        for index, (source, target) in enumerate(
            [(ids_in, ids_ref), (probs_in, probs_ref), (tokens_in, tokens_ref)]
        )
    ]
    for copy in copies:
        copy.start()
    for copy in copies:
        copy.wait()
    probs = probs_ref[...]
    weights = probs / jnp.sum(probs, axis=1, keepdims=True)
    shape = (rows_ref.shape[0], rows_ref.shape[1] - width)
    lane = lax.broadcasted_iota(jnp.int32, shape, 1)
    expert = jnp.where(lane < experts, lane, lane - experts)
    dense = jnp.zeros(shape, jnp.float32)
    for column in range(probs.shape[1]):
        chosen = ids_ref[:, column : column + 1] == expert
        dense = dense + jnp.where(chosen, weights[:, column : column + 1], 0.0)
    high = dense.astype(jnp.bfloat16).astype(jnp.float32)
    rows_ref[:, :width] = tokens_ref[...]
    rows_ref[:, width:] = jnp.where(lane < experts, high, dense - high).astype(jnp.bfloat16)


def chunk_of(refs, local_experts, per_block, index):
    gate_ref, up_ref, down_ref = refs
    block, place = divmod(index, 3 * per_block)
    if place < 2 * per_block:
        return (gate_ref, up_ref)[place % 2].at[block * per_block + place // 2]
    return down_ref.at[block * per_block + place - 2 * per_block]


def early_kernel(per_block, after_ref, gate_ref, up_ref, down_ref, early_ref, sem):
    copies = [
        pltpu.make_async_copy(
            chunk_of((gate_ref, up_ref, down_ref), gate_ref.shape[0], per_block, index), early_ref.at[index], sem.at[index]
        )
        for index in range(early_ref.shape[0])
    ]
    for copy in copies:
        copy.start()
    for copy in copies:
        copy.wait()


def expert_kernel(pieces, per_block, experts, parts, *refs):
    row_refs = refs[:pieces]
    early_ref, gate_ref, up_ref, down_ref, own_ref, kept_ref, sent_ref, rows, total, ring, ring_sem = refs[pieces:]
    local_experts, expert_hidden, width = gate_ref.shape
    tokens = rows.shape[0]
    early, slots, chunks = early_ref.shape[0], ring.shape[0], 3 * local_experts

    def fetch(index):
        slot = (index - early) % slots
        return pltpu.make_async_copy(
            chunk_of((gate_ref, up_ref, down_ref), local_experts, per_block, index), ring.at[slot], ring_sem.at[slot]
        )

    def chunk(index):
        if index < early:
            return early_ref.at[index]
        fetch(index).wait()
        return ring.at[(index - early) % slots]

    def used(index):
        if index >= early and index + slots < chunks:
            fetch(index + slots).start()

    for index in range(early, min(early + slots, chunks)):
        fetch(index).start()

    route = []
    held, start = [], 0
    for ref in row_refs:
        held.append(ref[...].astype(jnp.float32))
        count = sum(piece.shape[0] for piece in held)
        if count % PACK == 0:
            joined = jnp.concatenate(held, axis=0) if len(held) > 1 else held[0]
            rows[start : start + count, :] = joined[:, :width].astype(jnp.bfloat16)
            route.append(joined[:, width:])
            held, start = [], start + count
    route = jnp.concatenate(route, axis=0).astype(jnp.bfloat16)
    lane = lax.broadcasted_iota(jnp.int32, (local_experts, route.shape[1]), 1)
    wanted = lax.axis_index("expert") * local_experts + lax.broadcasted_iota(
        jnp.int32, (local_experts, route.shape[1]), 0
    )
    chooser = ((lane == wanted) | (lane == wanted + experts)).astype(jnp.bfloat16)
    weights = lax.dot_general(chooser, route, NT, preferred_element_type=jnp.float32)

    part = width // parts
    half = expert_hidden // 2
    for block in range(local_experts // per_block):
        first = block * 3 * per_block
        hidden = []
        for index in range(per_block):
            expert = block * per_block + index
            gate_at, up_at = first + 2 * index, first + 2 * index + 1
            weight_refs = [chunk(gate_at), chunk(up_at)]
            gate, up = [
                [
                    lax.dot_general(
                        ref[start : start + half, :], rows[...], NT, preferred_element_type=jnp.float32
                    )
                    for start in (0, half)
                ]
                for ref in weight_refs
            ]
            used(gate_at)
            used(up_at)
            for g, u in zip(gate, up):
                hidden.append(g / (1.0 + jnp.exp(-g)) * u * weights[expert : expert + 1, :])
        hidden = jnp.concatenate(hidden, axis=0).T.astype(jnp.bfloat16)
        if tokens < ROW_TILE:
            hidden = jnp.concatenate([hidden, jnp.zeros((ROW_TILE - tokens, hidden.shape[1]), jnp.bfloat16)], axis=0)
        downs = [chunk(first + 2 * per_block + index) for index in range(per_block)]
        for index in range(parts):
            columns = pl.ds(index * part, part)
            down = [ref[:, columns] for ref in downs]
            down = jnp.concatenate(down, axis=0) if per_block > 1 else down[0]
            product = jnp.dot(hidden, down, preferred_element_type=jnp.float32)[:tokens]
            if block:
                total[:, columns] += product
            else:
                total[:, columns] = product
        for index in range(per_block):
            used(first + 2 * per_block + index)

    chip = own_ref.shape[0]
    exclusive = kept_ref.shape[0] - chip
    own_ref[...] = total[:chip, :]
    kept_ref[:exclusive, :] = total[chip : chip + exclusive, :]
    kept_ref[exclusive:, :] = total[tokens - chip :, :]
    sent_ref[...] = jnp.concatenate(
        [total[chip + exclusive : tokens - chip, :], total[tokens - chip :, :]], axis=0
    ).astype(jnp.bfloat16)


def chip_sum_kernel(kept_ref, arrived_ref, *out_refs):
    summed = kept_ref[...] + arrived_ref[...].astype(jnp.float32)
    chip_rows = out_refs[0].shape[0]
    for index, out_ref in enumerate(out_refs[:-1]):
        out_ref[...] = summed[index * chip_rows : (index + 1) * chip_rows, :].astype(jnp.bfloat16)
    half = out_refs[-1].shape[0]
    rows = kept_ref.shape[0]
    arrived = arrived_ref[...].astype(jnp.float32)
    out_refs[-1][...] = (
        kept_ref[rows - 2 * half : rows - half, :] + arrived[rows - half :, :]
    ).astype(jnp.bfloat16)


def token_sum_kernel(own_ref, shared_ref, *refs):
    piece_refs, mine_ref, other_ref = refs[:-2], refs[-2], refs[-1]
    total = own_ref[...]
    for ref in piece_refs:
        total = total + ref[...].astype(jnp.float32)
    half = mine_ref.shape[0]
    mine_ref[...] = total[:half, :] + shared_ref[...].astype(jnp.float32)
    other_ref[...] = total[half:, :]


def last_kernel(mine_ref, other_ref, out_ref):
    out_ref[...] = (mine_ref[...] + other_ref[...]).astype(jnp.bfloat16)


def call(kernel, out_shapes, *args, name):
    held = sum(array.size * 4 for array in [*args, *jax.tree.leaves(out_shapes)])
    return pl.pallas_call(
        kernel,
        out_shape=out_shapes,
        in_specs=[VMEM] * len(args),
        out_specs=jax.tree.map(lambda _: VMEM, out_shapes),
        compiler_params=pltpu.CompilerParams(vmem_limit_bytes=2 * held + 2**20),
        name=name,
    )(*args)


def local(tokens, expert_ids, route_probs, gate_weight, up_weight, down_weight):
    own_rows, width = tokens.shape
    local_experts, expert_hidden, _ = gate_weight.shape
    experts = local_experts * lax.axis_size("expert")
    chips = lax.axis_size("expert") * lax.axis_size("rep") // 2
    pairs, shared = chip_pairs(chips)
    swap = core_perm(chips)
    all_rows = 2 * own_rows * chips
    chip_rows = 2 * own_rows
    reduced = chip_rows * (len(pairs) + 1)
    per_block = 2 if local_experts % 2 == 0 else 1
    chunk_bytes = expert_hidden * width * 2
    chunks = 3 * local_experts
    early = min(EARLY_CHUNKS, chunks - 1)
    parts = max(2, all_rows // 64)

    mine = pl.pallas_call(
        functools.partial(rows_kernel, experts),
        out_shape=jax.ShapeDtypeStruct((own_rows, width + padded_lanes(experts)), jnp.bfloat16),
        in_specs=[pl.BlockSpec(memory_space=pl.ANY)] * 3,
        out_specs=VMEM,
        scratch_shapes=[pltpu.VMEM(array.shape, array.dtype) for array in (tokens, expert_ids, route_probs)]
        + [pltpu.SemaphoreType.DMA((3,))],
        compiler_params=pltpu.CompilerParams(vmem_limit_bytes=VMEM_BYTES - 2**16),
        name="rows",
    )(tokens, expert_ids, route_probs)
    shared_rows = lax.ppermute(mine, LINKED, chip_perm(chips, shared, shared))
    both = jnp.concatenate([mine, lax.ppermute(mine, LINKED, swap)], axis=0)
    fetched = [lax.ppermute(both, LINKED, chip_perm(chips, *pair)) for pair in pairs]
    early_weights = pl.pallas_call(
        functools.partial(early_kernel, per_block),
        out_shape=pltpu.VMEM((early, expert_hidden, width), jnp.bfloat16),
        in_specs=[pl.BlockSpec(memory_space=pl.ANY)] + [HBM] * 3,
        out_specs=VMEM,
        scratch_shapes=[pltpu.SemaphoreType.DMA((early,))],
        compiler_params=pltpu.CompilerParams(vmem_limit_bytes=VMEM_BYTES - early * chunk_bytes - 20 * 2**20),
        cost_estimate=pl.CostEstimate(flops=0, bytes_accessed=2 * early * chunk_bytes, transcendentals=0),
        name="early_weights",
    )(both, gate_weight, up_weight, down_weight)
    passed = [lax.ppermute(rows, LINKED, swap) for rows in fetched]
    shared_passed = lax.ppermute(shared_rows, LINKED, swap)
    pieces = [in_vmem(piece) for piece in [both] + fetched + passed + [shared_rows, shared_passed]]

    scratch_bytes = all_rows * width * (2 + 4 + 2 + 2 + 1) + all_rows * (width // parts + 5 * per_block * expert_hidden) * 4
    slots = min(RING_CHUNKS, chunks - early, (VMEM_BYTES - early * chunk_bytes - scratch_bytes - 6 * 2**20) // chunk_bytes)
    own, kept, sent = pl.pallas_call(
        functools.partial(expert_kernel, len(pieces), per_block, experts, parts),
        out_shape=(
            jax.ShapeDtypeStruct((chip_rows, width), jnp.float32),
            jax.ShapeDtypeStruct((reduced, width), jnp.float32),
            jax.ShapeDtypeStruct((reduced, width), jnp.bfloat16),
        ),
        in_specs=[VMEM] * (len(pieces) + 1) + [HBM] * 3,
        out_specs=(VMEM, VMEM, VMEM),
        scratch_shapes=[
            pltpu.VMEM((all_rows, width), jnp.bfloat16),
            pltpu.VMEM((all_rows, width), jnp.float32),
            pltpu.VMEM((slots, expert_hidden, width), jnp.bfloat16),
            pltpu.SemaphoreType.DMA((slots,)),
        ],
        compiler_params=pltpu.CompilerParams(vmem_limit_bytes=scratch_bytes + slots * chunk_bytes + 3 * 2**20),
        cost_estimate=pl.CostEstimate(
            flops=6 * all_rows * local_experts * expert_hidden * width,
            bytes_accessed=chunks * chunk_bytes,
            transcendentals=all_rows * local_experts * expert_hidden,
        ),
        name="experts",
    )(*pieces, early_weights, gate_weight, up_weight, down_weight)

    summed = call(
        chip_sum_kernel,
        [jax.ShapeDtypeStruct((chip_rows, width), jnp.bfloat16)] * len(pairs)
        + [jax.ShapeDtypeStruct((own_rows, width), jnp.bfloat16)],
        in_vmem(kept),
        in_vmem(lax.ppermute(sent, LINKED, swap)),
        name="chip_sum",
    )
    returned = [lax.ppermute(rows, LINKED, chip_perm(chips, *pair)) for rows, pair in zip(summed, pairs)]
    shared_back = lax.ppermute(summed[-1], LINKED, chip_perm(chips, shared, shared))
    half = jax.ShapeDtypeStruct((own_rows, width), jnp.float32)
    own_part, other_part = call(
        token_sum_kernel,
        [half, half],
        *[in_vmem(array) for array in [own, shared_back] + returned],
        name="token_sum",
    )
    return call(
        last_kernel,
        jax.ShapeDtypeStruct((own_rows, width), jnp.bfloat16),
        own_part,
        lax.ppermute(other_part, LINKED, swap),
        name="last_sum",
    )


def solution(mesh):
    by_device = P(("groups", "expert", "rep"), None)
    by_expert = P("expert", "rep", None)
    return jax.shard_map(
        local,
        mesh=mesh,
        in_specs=(by_device,) * 3 + (by_expert,) * 3,
        out_specs=by_device,
        check_vma=False,
    )
```

```python
import functools

import jax
import jax.numpy as jnp
from jax import lax
from jax.experimental import pallas as pl
from jax.experimental.pallas import tpu as pltpu
from jax.sharding import PartitionSpec as P

LANES = 128
PACK = 16
ROW_TILE = 128
VMEM_BYTES = 64 * 2**20
EARLY_CHUNKS = 5
RING_CHUNKS = 10
NT = (((1,), (1,)), ((), ()))
LINKED = ("expert", "rep")
VMEM = pl.BlockSpec(memory_space=pltpu.VMEM)
HBM = pl.BlockSpec(memory_space=pltpu.HBM)


def chip_pairs(chips):
    return [(k + 1, k) if k + 2 == chips else (k, k + 1) for k in range(chips - 2, 0, -2)], 1


def chip_perm(chips, first, second):
    return [
        (chip * 2 + core, ((chip ^ (second if core else first)) << 1) | core)
        for chip in range(chips)
        for core in (0, 1)
    ]


def core_perm(chips):
    return [(device, device ^ 1) for device in range(2 * chips)]


def in_vmem(array):
    return pltpu.with_memory_space_constraint(array, pltpu.VMEM)


def padded_lanes(experts):
    return -(-2 * experts // LANES) * LANES


def rows_kernel(experts, tokens_in, ids_in, probs_in, rows_ref, tokens_ref, ids_ref, probs_ref, sem):
    width = tokens_ref.shape[1]
    copies = [
        pltpu.make_async_copy(source, target, sem.at[index])
        for index, (source, target) in enumerate(
            [(ids_in, ids_ref), (probs_in, probs_ref), (tokens_in, tokens_ref)]
        )
    ]
    for copy in copies:
        copy.start()
    for copy in copies:
        copy.wait()
    probs = probs_ref[...]
    weights = probs / jnp.sum(probs, axis=1, keepdims=True)
    shape = (rows_ref.shape[0], rows_ref.shape[1] - width)
    lane = lax.broadcasted_iota(jnp.int32, shape, 1)
    expert = jnp.where(lane < experts, lane, lane - experts)
    dense = jnp.zeros(shape, jnp.float32)
    for column in range(probs.shape[1]):
        chosen = ids_ref[:, column : column + 1] == expert
        dense = dense + jnp.where(chosen, weights[:, column : column + 1], 0.0)
    high = dense.astype(jnp.bfloat16).astype(jnp.float32)
    rows_ref[:, :width] = tokens_ref[...]
    rows_ref[:, width:] = jnp.where(lane < experts, high, dense - high).astype(jnp.bfloat16)


def chunk_of(refs, local_experts, per_block, index):
    gate_ref, up_ref, down_ref = refs
    block, place = divmod(index, 3 * per_block)
    if place < 2 * per_block:
        return (gate_ref, up_ref)[place % 2].at[block * per_block + place // 2]
    return down_ref.at[block * per_block + place - 2 * per_block]


def early_kernel(per_block, after_ref, gate_ref, up_ref, down_ref, early_ref, done_ref, sem):
    copies = [
        pltpu.make_async_copy(
            chunk_of((gate_ref, up_ref, down_ref), gate_ref.shape[0], per_block, index), early_ref.at[index], sem.at[index]
        )
        for index in range(early_ref.shape[0])
    ]
    for copy in copies:
        copy.start()
    for copy in copies:
        copy.wait()
    done_ref[...] = jnp.zeros_like(done_ref)


def expert_kernel(pieces, per_block, experts, parts, *refs):
    row_refs = refs[:pieces]
    _, early_ref, gate_ref, up_ref, down_ref, own_ref, kept_ref, sent_ref, rows, total, ring, ring_sem = refs[pieces:]
    local_experts, expert_hidden, width = gate_ref.shape
    tokens = rows.shape[0]
    early, slots, chunks = early_ref.shape[0], ring.shape[0], 3 * local_experts

    def fetch(index):
        slot = (index - early) % slots
        return pltpu.make_async_copy(
            chunk_of((gate_ref, up_ref, down_ref), local_experts, per_block, index), ring.at[slot], ring_sem.at[slot]
        )

    def chunk(index):
        if index < early:
            return early_ref.at[index]
        fetch(index).wait()
        return ring.at[(index - early) % slots]

    def used(index):
        if index >= early and index + slots < chunks:
            fetch(index + slots).start()

    for index in range(early, min(early + slots, chunks)):
        fetch(index).start()

    route = []
    held, start = [], 0
    for ref in row_refs:
        held.append(ref[...].astype(jnp.float32))
        count = sum(piece.shape[0] for piece in held)
        if count % PACK == 0:
            joined = jnp.concatenate(held, axis=0) if len(held) > 1 else held[0]
            rows[start : start + count, :] = joined[:, :width].astype(jnp.bfloat16)
            route.append(joined[:, width:])
            held, start = [], start + count
    route = jnp.concatenate(route, axis=0).astype(jnp.bfloat16)
    lane = lax.broadcasted_iota(jnp.int32, (local_experts, route.shape[1]), 1)
    wanted = lax.axis_index("expert") * local_experts + lax.broadcasted_iota(
        jnp.int32, (local_experts, route.shape[1]), 0
    )
    chooser = ((lane == wanted) | (lane == wanted + experts)).astype(jnp.bfloat16)
    weights = lax.dot_general(chooser, route, NT, preferred_element_type=jnp.float32)

    part = width // parts
    half = expert_hidden // 2
    for block in range(local_experts // per_block):
        first = block * 3 * per_block
        hidden = []
        for index in range(per_block):
            expert = block * per_block + index
            gate_at, up_at = first + 2 * index, first + 2 * index + 1
            weight_refs = [chunk(gate_at), chunk(up_at)]
            gate, up = [
                [
                    lax.dot_general(
                        ref[start : start + half, :], rows[...], NT, preferred_element_type=jnp.float32
                    )
                    for start in (0, half)
                ]
                for ref in weight_refs
            ]
            used(gate_at)
            used(up_at)
            for g, u in zip(gate, up):
                hidden.append(g / (1.0 + jnp.exp(-g)) * u * weights[expert : expert + 1, :])
        hidden = jnp.concatenate(hidden, axis=0).T.astype(jnp.bfloat16)
        if tokens < ROW_TILE:
            hidden = jnp.concatenate([hidden, jnp.zeros((ROW_TILE - tokens, hidden.shape[1]), jnp.bfloat16)], axis=0)
        downs = [chunk(first + 2 * per_block + index) for index in range(per_block)]
        for index in range(parts):
            columns = pl.ds(index * part, part)
            down = [ref[:, columns] for ref in downs]
            down = jnp.concatenate(down, axis=0) if per_block > 1 else down[0]
            product = jnp.dot(hidden, down, preferred_element_type=jnp.float32)[:tokens]
            if block:
                total[:, columns] += product
            else:
                total[:, columns] = product
        for index in range(per_block):
            used(first + 2 * per_block + index)

    chip = own_ref.shape[0]
    exclusive = kept_ref.shape[0] - chip
    own_ref[...] = total[:chip, :]
    kept_ref[:exclusive, :] = total[chip : chip + exclusive, :]
    kept_ref[exclusive:, :] = total[tokens - chip :, :]
    sent_ref[...] = jnp.concatenate(
        [total[chip + exclusive : tokens - chip, :], total[tokens - chip :, :]], axis=0
    ).astype(jnp.bfloat16)


def chip_sum_kernel(kept_ref, arrived_ref, *out_refs):
    summed = kept_ref[...] + arrived_ref[...].astype(jnp.float32)
    chip_rows = out_refs[0].shape[0]
    for index, out_ref in enumerate(out_refs[:-1]):
        out_ref[...] = summed[index * chip_rows : (index + 1) * chip_rows, :].astype(jnp.bfloat16)
    half = out_refs[-1].shape[0]
    rows = kept_ref.shape[0]
    arrived = arrived_ref[...].astype(jnp.float32)
    out_refs[-1][...] = (
        kept_ref[rows - 2 * half : rows - half, :] + arrived[rows - half :, :]
    ).astype(jnp.bfloat16)


def token_sum_kernel(own_ref, shared_ref, *refs):
    piece_refs, mine_ref, other_ref = refs[:-2], refs[-2], refs[-1]
    total = own_ref[...]
    for ref in piece_refs:
        total = total + ref[...].astype(jnp.float32)
    half = mine_ref.shape[0]
    mine_ref[...] = total[:half, :] + shared_ref[...].astype(jnp.float32)
    other_ref[...] = total[half:, :]


def last_kernel(mine_ref, other_ref, out_ref):
    out_ref[...] = (mine_ref[...] + other_ref[...]).astype(jnp.bfloat16)


def call(kernel, out_shapes, *args, name):
    held = sum(array.size * 4 for array in [*args, *jax.tree.leaves(out_shapes)])
    return pl.pallas_call(
        kernel,
        out_shape=out_shapes,
        in_specs=[VMEM] * len(args),
        out_specs=jax.tree.map(lambda _: VMEM, out_shapes),
        compiler_params=pltpu.CompilerParams(vmem_limit_bytes=2 * held + 2**20),
        name=name,
    )(*args)


def local(tokens, expert_ids, route_probs, gate_weight, up_weight, down_weight):
    own_rows, width = tokens.shape
    local_experts, expert_hidden, _ = gate_weight.shape
    experts = local_experts * lax.axis_size("expert")
    chips = lax.axis_size("expert") * lax.axis_size("rep") // 2
    pairs, shared = chip_pairs(chips)
    swap = core_perm(chips)
    all_rows = 2 * own_rows * chips
    chip_rows = 2 * own_rows
    reduced = chip_rows * (len(pairs) + 1)
    per_block = 2 if local_experts % 2 == 0 else 1
    chunk_bytes = expert_hidden * width * 2
    chunks = 3 * local_experts
    early = min(EARLY_CHUNKS, chunks - 1)
    parts = max(2, all_rows // 64)

    mine = pl.pallas_call(
        functools.partial(rows_kernel, experts),
        out_shape=jax.ShapeDtypeStruct((own_rows, width + padded_lanes(experts)), jnp.bfloat16),
        in_specs=[pl.BlockSpec(memory_space=pl.ANY)] * 3,
        out_specs=VMEM,
        scratch_shapes=[pltpu.VMEM(array.shape, array.dtype) for array in (tokens, expert_ids, route_probs)]
        + [pltpu.SemaphoreType.DMA((3,))],
        compiler_params=pltpu.CompilerParams(vmem_limit_bytes=VMEM_BYTES - 2**16),
        name="rows",
    )(tokens, expert_ids, route_probs)
    shared_rows = lax.ppermute(mine, LINKED, chip_perm(chips, shared, shared))
    both = jnp.concatenate([mine, lax.ppermute(mine, LINKED, swap)], axis=0)
    fetched = [lax.ppermute(both, LINKED, chip_perm(chips, *pair)) for pair in pairs]
    scratch_bytes = all_rows * width * (2 + 4 + 2 + 2 + 1) + all_rows * (width // parts + 5 * per_block * expert_hidden) * 4
    slots = min(RING_CHUNKS, chunks - early, (VMEM_BYTES - early * chunk_bytes - scratch_bytes - 6 * 2**20) // chunk_bytes)
    vmem_limit_bytes = scratch_bytes + slots * chunk_bytes + 3 * 2**20
    early_weights, early_done = pl.pallas_call(
        functools.partial(early_kernel, per_block),
        out_shape=(
            pltpu.VMEM((early, expert_hidden, width), jnp.bfloat16),
            jax.ShapeDtypeStruct((8, LANES), jnp.float32),
        ),
        in_specs=[pl.BlockSpec(memory_space=pl.ANY)] + [HBM] * 3,
        out_specs=(VMEM, VMEM),
        scratch_shapes=[pltpu.SemaphoreType.DMA((early,))],
        compiler_params=pltpu.CompilerParams(vmem_limit_bytes=vmem_limit_bytes),
        cost_estimate=pl.CostEstimate(flops=0, bytes_accessed=2 * early * chunk_bytes, transcendentals=0),
        name="early_weights",
    )(both, gate_weight, up_weight, down_weight)
    *fetched, early_done = lax.optimization_barrier((*fetched, early_done))
    passed = [lax.ppermute(rows, LINKED, swap) for rows in fetched]
    shared_passed = lax.ppermute(shared_rows, LINKED, swap)
    pieces = [in_vmem(piece) for piece in [both] + fetched + passed + [shared_rows, shared_passed]]

    own, kept, sent = pl.pallas_call(
        functools.partial(expert_kernel, len(pieces), per_block, experts, parts),
        out_shape=(
            jax.ShapeDtypeStruct((chip_rows, width), jnp.float32),
            jax.ShapeDtypeStruct((reduced, width), jnp.float32),
            jax.ShapeDtypeStruct((reduced, width), jnp.bfloat16),
        ),
        in_specs=[VMEM] * len(pieces) + [pl.BlockSpec(memory_space=pl.ANY), VMEM] + [HBM] * 3,
        out_specs=(VMEM, VMEM, VMEM),
        scratch_shapes=[
            pltpu.VMEM((all_rows, width), jnp.bfloat16),
            pltpu.VMEM((all_rows, width), jnp.float32),
            pltpu.VMEM((slots, expert_hidden, width), jnp.bfloat16),
            pltpu.SemaphoreType.DMA((slots,)),
        ],
        compiler_params=pltpu.CompilerParams(vmem_limit_bytes=vmem_limit_bytes),
        cost_estimate=pl.CostEstimate(
            flops=6 * all_rows * local_experts * expert_hidden * width,
            bytes_accessed=chunks * chunk_bytes,
            transcendentals=all_rows * local_experts * expert_hidden,
        ),
        name="experts",
    )(*pieces, early_done, early_weights, gate_weight, up_weight, down_weight)

    summed = call(
        chip_sum_kernel,
        [jax.ShapeDtypeStruct((chip_rows, width), jnp.bfloat16)] * len(pairs)
        + [jax.ShapeDtypeStruct((own_rows, width), jnp.bfloat16)],
        in_vmem(kept),
        in_vmem(lax.ppermute(sent, LINKED, swap)),
        name="chip_sum",
    )
    returned = [lax.ppermute(rows, LINKED, chip_perm(chips, *pair)) for rows, pair in zip(summed, pairs)]
    shared_back = lax.ppermute(summed[-1], LINKED, chip_perm(chips, shared, shared))
    half = jax.ShapeDtypeStruct((own_rows, width), jnp.float32)
    own_part, other_part = call(
        token_sum_kernel,
        [half, half],
        *[in_vmem(array) for array in [own, shared_back] + returned],
        name="token_sum",
    )
    return call(
        last_kernel,
        jax.ShapeDtypeStruct((own_rows, width), jnp.bfloat16),
        own_part,
        lax.ppermute(other_part, LINKED, swap),
        name="last_sum",
    )


def solution(mesh):
    by_device = P(("groups", "expert", "rep"), None)
    by_expert = P("expert", "rep", None)
    return jax.shard_map(
        local,
        mesh=mesh,
        in_specs=(by_device,) * 3 + (by_expert,) * 3,
        out_specs=by_device,
        check_vma=False,
    )
```

```python
import functools

import jax
import jax.numpy as jnp
from jax import lax
from jax.experimental import pallas as pl
from jax.experimental.pallas import tpu as pltpu
from jax.sharding import PartitionSpec as P

LANES = 128
PACK = 16
ROW_TILE = 128
VMEM_BYTES = 64 * 2**20
EARLY_CHUNKS = 5
RING_CHUNKS = 8
NT = (((1,), (1,)), ((), ()))
LINKED = ("expert", "rep")
VMEM = pl.BlockSpec(memory_space=pltpu.VMEM)
HBM = pl.BlockSpec(memory_space=pltpu.HBM)


def chip_pairs(chips):
    return [(k + 1, k) if k + 2 == chips else (k, k + 1) for k in range(chips - 2, 0, -2)], 1


def chip_perm(chips, first, second):
    return [
        (chip * 2 + core, ((chip ^ (second if core else first)) << 1) | core)
        for chip in range(chips)
        for core in (0, 1)
    ]


def core_perm(chips):
    return [(device, device ^ 1) for device in range(2 * chips)]


def in_vmem(array):
    return pltpu.with_memory_space_constraint(array, pltpu.VMEM)


def padded_lanes(experts):
    return -(-2 * experts // LANES) * LANES


def rows_kernel(experts, tokens_in, ids_in, probs_in, rows_ref, tokens_ref, ids_ref, probs_ref, sem):
    width = tokens_ref.shape[1]
    copies = [
        pltpu.make_async_copy(source, target, sem.at[index])
        for index, (source, target) in enumerate(
            [(ids_in, ids_ref), (probs_in, probs_ref), (tokens_in, tokens_ref)]
        )
    ]
    for copy in copies:
        copy.start()
    for copy in copies:
        copy.wait()
    probs = probs_ref[...]
    weights = probs / jnp.sum(probs, axis=1, keepdims=True)
    shape = (rows_ref.shape[0], rows_ref.shape[1] - width)
    lane = lax.broadcasted_iota(jnp.int32, shape, 1)
    expert = jnp.where(lane < experts, lane, lane - experts)
    dense = jnp.zeros(shape, jnp.float32)
    for column in range(probs.shape[1]):
        chosen = ids_ref[:, column : column + 1] == expert
        dense = dense + jnp.where(chosen, weights[:, column : column + 1], 0.0)
    high = dense.astype(jnp.bfloat16).astype(jnp.float32)
    rows_ref[:, :width] = tokens_ref[...]
    rows_ref[:, width:] = jnp.where(lane < experts, high, dense - high).astype(jnp.bfloat16)


def chunk_of(refs, local_experts, per_block, index):
    gate_ref, up_ref, down_ref = refs
    block, place = divmod(index, 3 * per_block)
    if place < 2 * per_block:
        return (gate_ref, up_ref)[place % 2].at[block * per_block + place // 2]
    return down_ref.at[block * per_block + place - 2 * per_block]


def early_kernel(per_block, after_ref, gate_ref, up_ref, down_ref, early_ref, done_ref, sem):
    copies = [
        pltpu.make_async_copy(
            chunk_of((gate_ref, up_ref, down_ref), gate_ref.shape[0], per_block, index), early_ref.at[index], sem.at[index]
        )
        for index in range(early_ref.shape[0])
    ]
    for copy in copies:
        copy.start()
    for copy in copies:
        copy.wait()
    done_ref[...] = jnp.zeros_like(done_ref)


def expert_kernel(pieces, per_block, experts, parts, *refs):
    row_refs = refs[:pieces]
    _, early_ref, gate_ref, up_ref, down_ref, own_ref, kept_ref, sent_ref, rows, total, ring, ring_sem = refs[pieces:]
    local_experts, expert_hidden, width = gate_ref.shape
    tokens = rows.shape[0]
    early, slots, chunks = early_ref.shape[0], ring.shape[0], 3 * local_experts

    def fetch(index):
        slot = (index - early) % slots
        return pltpu.make_async_copy(
            chunk_of((gate_ref, up_ref, down_ref), local_experts, per_block, index), ring.at[slot], ring_sem.at[slot]
        )

    def chunk(index):
        if index < early:
            return early_ref.at[index]
        fetch(index).wait()
        return ring.at[(index - early) % slots]

    def used(index):
        if index >= early and index + slots < chunks:
            fetch(index + slots).start()

    for index in range(early, min(early + slots, chunks)):
        fetch(index).start()

    route = []
    held, start = [], 0
    for ref in row_refs:
        held.append(ref[...].astype(jnp.float32))
        count = sum(piece.shape[0] for piece in held)
        if count % PACK == 0:
            joined = jnp.concatenate(held, axis=0) if len(held) > 1 else held[0]
            rows[start : start + count, :] = joined[:, :width].astype(jnp.bfloat16)
            route.append(joined[:, width:])
            held, start = [], start + count
    route = jnp.concatenate(route, axis=0).astype(jnp.bfloat16)
    lane = lax.broadcasted_iota(jnp.int32, (local_experts, route.shape[1]), 1)
    wanted = lax.axis_index("expert") * local_experts + lax.broadcasted_iota(
        jnp.int32, (local_experts, route.shape[1]), 0
    )
    chooser = ((lane == wanted) | (lane == wanted + experts)).astype(jnp.bfloat16)
    weights = lax.dot_general(chooser, route, NT, preferred_element_type=jnp.float32)

    part = width // parts
    half = expert_hidden // 2
    for block in range(local_experts // per_block):
        first = block * 3 * per_block
        hidden = []
        for index in range(per_block):
            expert = block * per_block + index
            gate_at, up_at = first + 2 * index, first + 2 * index + 1
            weight_refs = [chunk(gate_at), chunk(up_at)]
            gate, up = [
                [
                    lax.dot_general(
                        ref[start : start + half, :], rows[...], NT, preferred_element_type=jnp.float32
                    )
                    for start in (0, half)
                ]
                for ref in weight_refs
            ]
            used(gate_at)
            used(up_at)
            for g, u in zip(gate, up):
                hidden.append(g / (1.0 + jnp.exp(-g)) * u * weights[expert : expert + 1, :])
        hidden = jnp.concatenate(hidden, axis=0).T.astype(jnp.bfloat16)
        if tokens < ROW_TILE:
            hidden = jnp.concatenate([hidden, jnp.zeros((ROW_TILE - tokens, hidden.shape[1]), jnp.bfloat16)], axis=0)
        downs = [chunk(first + 2 * per_block + index) for index in range(per_block)]
        for index in range(parts):
            columns = pl.ds(index * part, part)
            down = [ref[:, columns] for ref in downs]
            down = jnp.concatenate(down, axis=0) if per_block > 1 else down[0]
            product = jnp.dot(hidden, down, preferred_element_type=jnp.float32)[:tokens]
            if block:
                total[:, columns] += product
            else:
                total[:, columns] = product
        for index in range(per_block):
            used(first + 2 * per_block + index)

    chip = own_ref.shape[0]
    exclusive = kept_ref.shape[0] - chip
    own_ref[...] = total[:chip, :]
    kept_ref[:exclusive, :] = total[chip : chip + exclusive, :]
    kept_ref[exclusive:, :] = total[tokens - chip :, :]
    sent_ref[...] = jnp.concatenate(
        [total[chip + exclusive : tokens - chip, :], total[tokens - chip :, :]], axis=0
    ).astype(jnp.bfloat16)


def chip_sum_kernel(kept_ref, arrived_ref, *out_refs):
    summed = kept_ref[...] + arrived_ref[...].astype(jnp.float32)
    chip_rows = out_refs[0].shape[0]
    for index, out_ref in enumerate(out_refs[:-1]):
        out_ref[...] = summed[index * chip_rows : (index + 1) * chip_rows, :].astype(jnp.bfloat16)
    half = out_refs[-1].shape[0]
    rows = kept_ref.shape[0]
    arrived = arrived_ref[...].astype(jnp.float32)
    out_refs[-1][...] = (
        kept_ref[rows - 2 * half : rows - half, :] + arrived[rows - half :, :]
    ).astype(jnp.bfloat16)


def token_sum_kernel(own_ref, shared_ref, *refs):
    piece_refs, mine_ref, other_ref = refs[:-2], refs[-2], refs[-1]
    total = own_ref[...]
    for ref in piece_refs:
        total = total + ref[...].astype(jnp.float32)
    half = mine_ref.shape[0]
    mine_ref[...] = total[:half, :] + shared_ref[...].astype(jnp.float32)
    other_ref[...] = total[half:, :]


def last_kernel(mine_ref, other_ref, out_ref):
    out_ref[...] = (mine_ref[...] + other_ref[...]).astype(jnp.bfloat16)


def call(kernel, out_shapes, *args, name):
    held = sum(array.size * 4 for array in [*args, *jax.tree.leaves(out_shapes)])
    return pl.pallas_call(
        kernel,
        out_shape=out_shapes,
        in_specs=[VMEM] * len(args),
        out_specs=jax.tree.map(lambda _: VMEM, out_shapes),
        compiler_params=pltpu.CompilerParams(vmem_limit_bytes=2 * held + 2**20),
        name=name,
    )(*args)


def local(tokens, expert_ids, route_probs, gate_weight, up_weight, down_weight):
    own_rows, width = tokens.shape
    local_experts, expert_hidden, _ = gate_weight.shape
    experts = local_experts * lax.axis_size("expert")
    chips = lax.axis_size("expert") * lax.axis_size("rep") // 2
    pairs, shared = chip_pairs(chips)
    swap = core_perm(chips)
    all_rows = 2 * own_rows * chips
    chip_rows = 2 * own_rows
    reduced = chip_rows * (len(pairs) + 1)
    per_block = 2 if local_experts % 2 == 0 else 1
    chunk_bytes = expert_hidden * width * 2
    chunks = 3 * local_experts
    early = min(EARLY_CHUNKS, chunks - 1)
    parts = max(2, all_rows // 64)

    mine = pl.pallas_call(
        functools.partial(rows_kernel, experts),
        out_shape=jax.ShapeDtypeStruct((own_rows, width + padded_lanes(experts)), jnp.bfloat16),
        in_specs=[pl.BlockSpec(memory_space=pl.ANY)] * 3,
        out_specs=VMEM,
        scratch_shapes=[pltpu.VMEM(array.shape, array.dtype) for array in (tokens, expert_ids, route_probs)]
        + [pltpu.SemaphoreType.DMA((3,))],
        compiler_params=pltpu.CompilerParams(vmem_limit_bytes=2**22),
        name="rows",
    )(*[pltpu.with_memory_space_constraint(array, pltpu.HBM) for array in (tokens, expert_ids, route_probs)])
    shared_rows = lax.ppermute(mine, LINKED, chip_perm(chips, shared, shared))
    both = jnp.concatenate([mine, lax.ppermute(mine, LINKED, swap)], axis=0)
    fetched = [lax.ppermute(both, LINKED, chip_perm(chips, *pair)) for pair in pairs]
    scratch_bytes = all_rows * width * (2 + 4 + 2 + 2 + 1) + all_rows * (width // parts + 5 * per_block * expert_hidden) * 4
    slots = min(RING_CHUNKS, chunks - early, (VMEM_BYTES - early * chunk_bytes - scratch_bytes - 6 * 2**20) // chunk_bytes)
    vmem_limit_bytes = scratch_bytes + slots * chunk_bytes + 3 * 2**20
    early_weights, early_done = pl.pallas_call(
        functools.partial(early_kernel, per_block),
        out_shape=(
            pltpu.VMEM((early, expert_hidden, width), jnp.bfloat16),
            jax.ShapeDtypeStruct((8, LANES), jnp.float32),
        ),
        in_specs=[pl.BlockSpec(memory_space=pl.ANY)] + [HBM] * 3,
        out_specs=(VMEM, VMEM),
        scratch_shapes=[pltpu.SemaphoreType.DMA((early,))],
        compiler_params=pltpu.CompilerParams(vmem_limit_bytes=vmem_limit_bytes),
        cost_estimate=pl.CostEstimate(flops=0, bytes_accessed=2 * early * chunk_bytes, transcendentals=0),
        name="early_weights",
    )(both, gate_weight, up_weight, down_weight)
    *fetched, early_done = lax.optimization_barrier((*fetched, early_done))
    passed = [lax.ppermute(rows, LINKED, swap) for rows in fetched]
    shared_passed = lax.ppermute(shared_rows, LINKED, swap)
    pieces = [in_vmem(piece) for piece in [both] + fetched + passed + [shared_rows, shared_passed]]

    own, kept, sent = pl.pallas_call(
        functools.partial(expert_kernel, len(pieces), per_block, experts, parts),
        out_shape=(
            jax.ShapeDtypeStruct((chip_rows, width), jnp.float32),
            jax.ShapeDtypeStruct((reduced, width), jnp.float32),
            jax.ShapeDtypeStruct((reduced, width), jnp.bfloat16),
        ),
        in_specs=[VMEM] * len(pieces) + [pl.BlockSpec(memory_space=pl.ANY), VMEM] + [HBM] * 3,
        out_specs=(VMEM, VMEM, VMEM),
        scratch_shapes=[
            pltpu.VMEM((all_rows, width), jnp.bfloat16),
            pltpu.VMEM((all_rows, width), jnp.float32),
            pltpu.VMEM((slots, expert_hidden, width), jnp.bfloat16),
            pltpu.SemaphoreType.DMA((slots,)),
        ],
        compiler_params=pltpu.CompilerParams(vmem_limit_bytes=vmem_limit_bytes),
        cost_estimate=pl.CostEstimate(
            flops=6 * all_rows * local_experts * expert_hidden * width,
            bytes_accessed=chunks * chunk_bytes,
            transcendentals=all_rows * local_experts * expert_hidden,
        ),
        name="experts",
    )(*pieces, early_done, early_weights, gate_weight, up_weight, down_weight)

    summed = call(
        chip_sum_kernel,
        [jax.ShapeDtypeStruct((chip_rows, width), jnp.bfloat16)] * len(pairs)
        + [jax.ShapeDtypeStruct((own_rows, width), jnp.bfloat16)],
        in_vmem(kept),
        in_vmem(lax.ppermute(sent, LINKED, swap)),
        name="chip_sum",
    )
    returned = [lax.ppermute(rows, LINKED, chip_perm(chips, *pair)) for rows, pair in zip(summed, pairs)]
    shared_back = lax.ppermute(summed[-1], LINKED, chip_perm(chips, shared, shared))
    half = jax.ShapeDtypeStruct((own_rows, width), jnp.float32)
    own_part, other_part = call(
        token_sum_kernel,
        [half, half],
        *[in_vmem(array) for array in [own, shared_back] + returned],
        name="token_sum",
    )
    return call(
        last_kernel,
        jax.ShapeDtypeStruct((own_rows, width), jnp.bfloat16),
        own_part,
        lax.ppermute(other_part, LINKED, swap),
        name="last_sum",
    )


def solution(mesh):
    by_device = P(("groups", "expert", "rep"), None)
    by_expert = P("expert", "rep", None)
    return jax.shard_map(
        local,
        mesh=mesh,
        in_specs=(by_device,) * 3 + (by_expert,) * 3,
        out_specs=by_device,
        check_vma=False,
    )
```

```python
import functools

import jax
import jax.numpy as jnp
from jax import lax
from jax.experimental import pallas as pl
from jax.experimental.pallas import tpu as pltpu
from jax.sharding import PartitionSpec as P

LANES = 128
PACK = 16
ROW_TILE = 128
VMEM_BYTES = 64 * 2**20
EARLY_CHUNKS = 5
RING_CHUNKS = 8
NT = (((1,), (1,)), ((), ()))
LINKED = ("expert", "rep")
VMEM = pl.BlockSpec(memory_space=pltpu.VMEM)
HBM = pl.BlockSpec(memory_space=pltpu.HBM)


def chip_pairs(chips):
    return [(k + 1, k) if k + 2 == chips else (k, k + 1) for k in range(chips - 2, 0, -2)], 1


def chip_perm(chips, first, second):
    return [
        (chip * 2 + core, ((chip ^ (second if core else first)) << 1) | core)
        for chip in range(chips)
        for core in (0, 1)
    ]


def core_perm(chips):
    return [(device, device ^ 1) for device in range(2 * chips)]


def in_vmem(array):
    return pltpu.with_memory_space_constraint(array, pltpu.VMEM)


def padded_lanes(experts):
    return -(-2 * experts // LANES) * LANES


def rows_kernel(experts, tokens_in, ids_in, probs_in, rows_ref, ids_ref, probs_ref, sem):
    width = tokens_in.shape[1]
    copies = [
        pltpu.make_async_copy(source, target, sem.at[index])
        for index, (source, target) in enumerate(
            [(ids_in, ids_ref), (probs_in, probs_ref), (tokens_in, rows_ref.at[:, pl.ds(0, width)])]
        )
    ]
    for copy in copies:
        copy.start()
    for copy in copies[:2]:
        copy.wait()
    probs = probs_ref[...]
    weights = probs / jnp.sum(probs, axis=1, keepdims=True)
    shape = (rows_ref.shape[0], rows_ref.shape[1] - width)
    lane = lax.broadcasted_iota(jnp.int32, shape, 1)
    expert = jnp.where(lane < experts, lane, lane - experts)
    dense = jnp.zeros(shape, jnp.float32)
    for column in range(probs.shape[1]):
        chosen = ids_ref[:, column : column + 1] == expert
        dense = dense + jnp.where(chosen, weights[:, column : column + 1], 0.0)
    high = dense.astype(jnp.bfloat16).astype(jnp.float32)
    rows_ref[:, width:] = jnp.where(lane < experts, high, dense - high).astype(jnp.bfloat16)
    copies[2].wait()


def chunk_of(refs, local_experts, per_block, index):
    gate_ref, up_ref, down_ref = refs
    block, place = divmod(index, 3 * per_block)
    if place < 2 * per_block:
        return (gate_ref, up_ref)[place % 2].at[block * per_block + place // 2]
    return down_ref.at[block * per_block + place - 2 * per_block]


def early_kernel(per_block, after_ref, gate_ref, up_ref, down_ref, early_ref, done_ref, sem):
    copies = [
        pltpu.make_async_copy(
            chunk_of((gate_ref, up_ref, down_ref), gate_ref.shape[0], per_block, index), early_ref.at[index], sem.at[index]
        )
        for index in range(early_ref.shape[0])
    ]
    for copy in copies:
        copy.start()
    for copy in copies:
        copy.wait()
    done_ref[...] = jnp.zeros_like(done_ref)


def expert_kernel(pieces, per_block, experts, parts, *refs):
    row_refs = refs[:pieces]
    _, early_ref, gate_ref, up_ref, down_ref, own_ref, kept_ref, sent_ref, rows, total, ring, ring_sem = refs[pieces:]
    local_experts, expert_hidden, width = gate_ref.shape
    tokens = rows.shape[0]
    early, slots, chunks = early_ref.shape[0], ring.shape[0], 3 * local_experts

    def fetch(index):
        slot = (index - early) % slots
        return pltpu.make_async_copy(
            chunk_of((gate_ref, up_ref, down_ref), local_experts, per_block, index), ring.at[slot], ring_sem.at[slot]
        )

    def chunk(index):
        if index < early:
            return early_ref.at[index]
        fetch(index).wait()
        return ring.at[(index - early) % slots]

    def used(index):
        if index >= early and index + slots < chunks:
            fetch(index + slots).start()

    for index in range(early, min(early + slots, chunks)):
        fetch(index).start()

    route = []
    held, start = [], 0
    for ref in row_refs:
        held.append(ref[...].astype(jnp.float32))
        count = sum(piece.shape[0] for piece in held)
        if count % PACK == 0:
            joined = jnp.concatenate(held, axis=0) if len(held) > 1 else held[0]
            rows[start : start + count, :] = joined[:, :width].astype(jnp.bfloat16)
            route.append(joined[:, width:])
            held, start = [], start + count
    route = jnp.concatenate(route, axis=0).astype(jnp.bfloat16)
    lane = lax.broadcasted_iota(jnp.int32, (local_experts, route.shape[1]), 1)
    wanted = lax.axis_index("expert") * local_experts + lax.broadcasted_iota(
        jnp.int32, (local_experts, route.shape[1]), 0
    )
    chooser = ((lane == wanted) | (lane == wanted + experts)).astype(jnp.bfloat16)
    weights = lax.dot_general(chooser, route, NT, preferred_element_type=jnp.float32)

    part = width // parts
    half = expert_hidden // 2
    for block in range(local_experts // per_block):
        first = block * 3 * per_block
        hidden = []
        for index in range(per_block):
            expert = block * per_block + index
            gate_at, up_at = first + 2 * index, first + 2 * index + 1
            weight_refs = [chunk(gate_at), chunk(up_at)]
            gate, up = [
                [
                    lax.dot_general(
                        ref[start : start + half, :], rows[...], NT, preferred_element_type=jnp.float32
                    )
                    for start in (0, half)
                ]
                for ref in weight_refs
            ]
            used(gate_at)
            used(up_at)
            for g, u in zip(gate, up):
                hidden.append(g / (1.0 + jnp.exp(-g)) * u * weights[expert : expert + 1, :])
        hidden = jnp.concatenate(hidden, axis=0).T.astype(jnp.bfloat16)
        if tokens < ROW_TILE:
            hidden = jnp.concatenate([hidden, jnp.zeros((ROW_TILE - tokens, hidden.shape[1]), jnp.bfloat16)], axis=0)
        downs = [chunk(first + 2 * per_block + index) for index in range(per_block)]
        for index in range(parts):
            columns = pl.ds(index * part, part)
            down = [ref[:, columns] for ref in downs]
            down = jnp.concatenate(down, axis=0) if per_block > 1 else down[0]
            product = jnp.dot(hidden, down, preferred_element_type=jnp.float32)[:tokens]
            if block:
                total[:, columns] += product
            else:
                total[:, columns] = product
        for index in range(per_block):
            used(first + 2 * per_block + index)

    chip = own_ref.shape[0]
    exclusive = kept_ref.shape[0] - chip
    own_ref[...] = total[:chip, :]
    kept_ref[:exclusive, :] = total[chip : chip + exclusive, :]
    kept_ref[exclusive:, :] = total[tokens - chip :, :]
    sent_ref[...] = jnp.concatenate(
        [total[chip + exclusive : tokens - chip, :], total[tokens - chip :, :]], axis=0
    ).astype(jnp.bfloat16)


def chip_sum_kernel(kept_ref, arrived_ref, *out_refs):
    summed = kept_ref[...] + arrived_ref[...].astype(jnp.float32)
    chip_rows = out_refs[0].shape[0]
    for index, out_ref in enumerate(out_refs[:-1]):
        out_ref[...] = summed[index * chip_rows : (index + 1) * chip_rows, :].astype(jnp.bfloat16)
    half = out_refs[-1].shape[0]
    rows = kept_ref.shape[0]
    arrived = arrived_ref[...].astype(jnp.float32)
    out_refs[-1][...] = (
        kept_ref[rows - 2 * half : rows - half, :] + arrived[rows - half :, :]
    ).astype(jnp.bfloat16)


def token_sum_kernel(own_ref, *refs):
    piece_refs, mine_ref, other_ref = refs[:-2], refs[-2], refs[-1]
    total = own_ref[...]
    for ref in piece_refs:
        total = total + ref[...].astype(jnp.float32)
    half = mine_ref.shape[0]
    mine_ref[...] = total[:half, :]
    other_ref[...] = total[half:, :]


def last_kernel(mine_ref, shared_ref, other_ref, out_ref):
    total = mine_ref[...] + shared_ref[...].astype(jnp.float32)
    out_ref[...] = (total + other_ref[...]).astype(jnp.bfloat16)


def call(kernel, out_shapes, *args, name):
    held = sum(array.size * 4 for array in [*args, *jax.tree.leaves(out_shapes)])
    return pl.pallas_call(
        kernel,
        out_shape=out_shapes,
        in_specs=[VMEM] * len(args),
        out_specs=jax.tree.map(lambda _: VMEM, out_shapes),
        compiler_params=pltpu.CompilerParams(vmem_limit_bytes=2 * held + 2**20),
        name=name,
    )(*args)


def local(tokens, expert_ids, route_probs, gate_weight, up_weight, down_weight):
    own_rows, width = tokens.shape
    local_experts, expert_hidden, _ = gate_weight.shape
    experts = local_experts * lax.axis_size("expert")
    chips = lax.axis_size("expert") * lax.axis_size("rep") // 2
    pairs, shared = chip_pairs(chips)
    swap = core_perm(chips)
    all_rows = 2 * own_rows * chips
    chip_rows = 2 * own_rows
    reduced = chip_rows * (len(pairs) + 1)
    per_block = 2 if local_experts % 2 == 0 else 1
    chunk_bytes = expert_hidden * width * 2
    chunks = 3 * local_experts
    early = min(EARLY_CHUNKS, chunks - 1)
    parts = max(2, all_rows // 64)

    mine = pl.pallas_call(
        functools.partial(rows_kernel, experts),
        out_shape=jax.ShapeDtypeStruct((own_rows, width + padded_lanes(experts)), jnp.bfloat16),
        in_specs=[pl.BlockSpec(memory_space=pl.ANY)] * 3,
        out_specs=VMEM,
        scratch_shapes=[pltpu.VMEM(array.shape, array.dtype) for array in (expert_ids, route_probs)]
        + [pltpu.SemaphoreType.DMA((3,))],
        compiler_params=pltpu.CompilerParams(vmem_limit_bytes=2**22),
        name="rows",
    )(*[pltpu.with_memory_space_constraint(array, pltpu.HBM) for array in (tokens, expert_ids, route_probs)])
    shared_rows = lax.ppermute(mine, LINKED, chip_perm(chips, shared, shared))
    both = jnp.concatenate([mine, lax.ppermute(mine, LINKED, swap)], axis=0)
    fetched = [lax.ppermute(both, LINKED, chip_perm(chips, *pair)) for pair in pairs]
    scratch_bytes = all_rows * width * (2 + 4 + 2 + 2 + 1) + all_rows * (width // parts + 5 * per_block * expert_hidden) * 4
    slots = min(RING_CHUNKS, chunks - early, (VMEM_BYTES - early * chunk_bytes - scratch_bytes - 6 * 2**20) // chunk_bytes)
    vmem_limit_bytes = scratch_bytes + slots * chunk_bytes + 3 * 2**20
    early_weights, early_done = pl.pallas_call(
        functools.partial(early_kernel, per_block),
        out_shape=(
            pltpu.VMEM((early, expert_hidden, width), jnp.bfloat16),
            jax.ShapeDtypeStruct((8, LANES), jnp.float32),
        ),
        in_specs=[pl.BlockSpec(memory_space=pl.ANY)] + [HBM] * 3,
        out_specs=(VMEM, VMEM),
        scratch_shapes=[pltpu.SemaphoreType.DMA((early,))],
        compiler_params=pltpu.CompilerParams(vmem_limit_bytes=vmem_limit_bytes),
        cost_estimate=pl.CostEstimate(flops=0, bytes_accessed=2 * early * chunk_bytes, transcendentals=0),
        name="early_weights",
    )(both, gate_weight, up_weight, down_weight)
    *fetched, early_done = lax.optimization_barrier((*fetched, early_done))
    passed = [lax.ppermute(rows, LINKED, swap) for rows in fetched]
    shared_passed = lax.ppermute(shared_rows, LINKED, swap)
    pieces = [in_vmem(piece) for piece in [both] + fetched + passed + [shared_rows, shared_passed]]

    own, kept, sent = pl.pallas_call(
        functools.partial(expert_kernel, len(pieces), per_block, experts, parts),
        out_shape=(
            jax.ShapeDtypeStruct((chip_rows, width), jnp.float32),
            jax.ShapeDtypeStruct((reduced, width), jnp.float32),
            jax.ShapeDtypeStruct((reduced, width), jnp.bfloat16),
        ),
        in_specs=[VMEM] * len(pieces) + [pl.BlockSpec(memory_space=pl.ANY), VMEM] + [HBM] * 3,
        out_specs=(VMEM, VMEM, VMEM),
        scratch_shapes=[
            pltpu.VMEM((all_rows, width), jnp.bfloat16),
            pltpu.VMEM((all_rows, width), jnp.float32),
            pltpu.VMEM((slots, expert_hidden, width), jnp.bfloat16),
            pltpu.SemaphoreType.DMA((slots,)),
        ],
        compiler_params=pltpu.CompilerParams(vmem_limit_bytes=vmem_limit_bytes),
        cost_estimate=pl.CostEstimate(
            flops=6 * all_rows * local_experts * expert_hidden * width,
            bytes_accessed=chunks * chunk_bytes,
            transcendentals=all_rows * local_experts * expert_hidden,
        ),
        name="experts",
    )(*pieces, early_done, early_weights, gate_weight, up_weight, down_weight)

    summed = call(
        chip_sum_kernel,
        [jax.ShapeDtypeStruct((chip_rows, width), jnp.bfloat16)] * len(pairs)
        + [jax.ShapeDtypeStruct((own_rows, width), jnp.bfloat16)],
        in_vmem(kept),
        in_vmem(lax.ppermute(sent, LINKED, swap)),
        name="chip_sum",
    )
    returned = [lax.ppermute(rows, LINKED, chip_perm(chips, *pair)) for rows, pair in zip(summed, pairs)]
    shared_back = lax.ppermute(summed[-1], LINKED, chip_perm(chips, shared, shared))
    half = jax.ShapeDtypeStruct((own_rows, width), jnp.float32)
    own_part, other_part = call(
        token_sum_kernel,
        [half, half],
        *[in_vmem(array) for array in [own] + returned],
        name="token_sum",
    )
    return call(
        last_kernel,
        jax.ShapeDtypeStruct((own_rows, width), jnp.bfloat16),
        own_part,
        shared_back,
        lax.ppermute(other_part, LINKED, swap),
        name="last_sum",
    )


def solution(mesh):
    by_device = P(("groups", "expert", "rep"), None)
    by_expert = P("expert", "rep", None)
    return jax.shard_map(
        local,
        mesh=mesh,
        in_specs=(by_device,) * 3 + (by_expert,) * 3,
        out_specs=by_device,
        check_vma=False,
    )
```
